32 devices in a mesh: leaf: 8 (over z, x), panel: 4 (over y, core).
Axes of the slice: x: 2, y: 2, z: 4, core: 2. Of those that a mesh axis runs over, the one named last changes fastest.
Arguments:
- child_front: float32 [8, 2048, 2048], P('leaf', 'panel'), as said below
- child_panel: bfloat16 [8, 2048, 4096], P('leaf'), may hold values from -0.03125 to 0.03125
- parent_front: float32 [4096, 4096], P('leaf', 'panel'), as said below
- tile_map: int32 [8, 8], P('leaf'), may hold values from 0 to 15, as said below
- tile_count: int32 [8], P('leaf'), may hold values from 2 to 8, as said below
Outputs:
- eliminated: float32 [4096, 4096], P('leaf', 'panel')
The draws below stay inside these ranges and needn't reach their ends.
Inputs may be any that keep to these rules, and one draw needn't show every extreme that they name: `tile_count`: some child has 8 live tiles and some child has 2. `tile_map`: for child c the first tile_count[c] entries are distinct and rising; the other entries are 0. Each child's block is symmetric, and child_front[c] - child_panel[c] child_panel[c]^T is positive definite. `parent_front`: symmetric positive definite.
All inputs are finite; a program needn't handle non-finite values.
Results may differ from the reference program's by a relative error of at most 0.0003.
Values sent between devices are 32-bit elements; how exact they have to be, the bound alone decides.
A program may use at most 128 MiB of HBM per device.

```python
import math
import jax
import jax.numpy as jnp
from jax import lax

TILE = 256
NF = 4096
CB = 2048
PC = 4096
STEPS = 4
CT = 8
FT = 16
CHILDREN = 8


kernel_reach = 0.1


def screened_matrix(key, lead, order, amplitude, lowest, highest, place_top, scale_low, scale_high):
    key_place, key_scale, key_diag = jax.random.split(key, 3)
    shape = lead + (order,)
    places = jax.random.uniform(key_place, shape, jnp.float32, 0.0, place_top)
    scales = jnp.exp(jax.random.uniform(key_scale, shape, jnp.float32, math.log(scale_low), math.log(scale_high)))
    diag_values = jnp.exp(jax.random.uniform(key_diag, shape, jnp.float32, math.log(lowest), math.log(highest)))
    distance = jnp.abs(places[..., :, None] - places[..., None, :])
    coupling = amplitude * scales[..., :, None] * scales[..., None, :] * jnp.exp(-distance / kernel_reach)
    on_diagonal = jnp.arange(order)[:, None] == jnp.arange(order)[None, :]
    return jnp.where(on_diagonal, coupling + diag_values[..., :, None], coupling)


def draw_child_front(key, part):
    base = jax.random.fold_in(key, 3)
    return screened_matrix(base, (CHILDREN,), CB, 2.0, 1.2, 2.4, 1.0, 0.75, 1.33)


def draw_parent_front(key, part):
    base = jax.random.fold_in(key, 5)
    return screened_matrix(base, (), NF, 2.0, 1.0, 2.0, 1.0, 0.75, 1.33)


def tile_layout(key):
    base = jax.random.fold_in(key, 41)
    key_count, key_pick, key_order = jax.random.split(base, 3)
    counts = jax.random.randint(key_count, (CHILDREN,), 2, CT + 1)
    picked = jax.random.permutation(key_pick, CHILDREN)
    counts = counts.at[picked[0]].set(CT).at[picked[1]].set(2)
    scores = jax.random.randint(key_order, (CHILDREN, FT), 0, 2 ** 20) * FT + jnp.arange(FT)[None, :]
    shuffled = jnp.argsort(scores, axis=1, stable=True)[:, :CT]
    position = jnp.arange(CT)[None, :]
    live_tiles = position < counts[:, None]
    scored = jnp.where(live_tiles, shuffled, FT + position)
    ordered = jnp.sort(scored, axis=1)
    maps = jnp.where(live_tiles, ordered, 0)
    return (maps.astype(jnp.int32), counts.astype(jnp.int32))


def draw_tile_map(key, part):
    return tile_layout(key)[0]


def draw_tile_count(key, part):
    return tile_layout(key)[1]


def block_scale(key, dims, cuts, least, high):
    gain, own = 1.0, jax.random.fold_in(key, 6)
    for dim, parts in cuts:
        steps = jnp.exp(jax.random.uniform(jax.random.fold_in(own, dim), (parts,), jnp.float32, least / len(cuts), high / len(cuts)))
        gain = gain * jnp.repeat(steps, dims[dim] // parts).reshape([-1 if axis == dim else 1 for axis in range(len(dims))])
    return gain


def noise(stream_key, shape, deviation, bound, cuts=(), kind=jnp.bfloat16):
    drawn = deviation * jax.random.normal(stream_key, shape, jnp.float32)
    if cuts:
        drawn = drawn * block_scale(stream_key, shape, cuts, -0.22, 0.18)
    return jnp.clip(drawn, -bound, bound).astype(kind)


def setup_inputs(seed: int = 0) -> dict:
    streams_of = jax.random.split(jax.random.key(seed), 6)
    return {
        "child_front": draw_child_front(jax.random.fold_in(streams_of[5], 71), 0),
        "child_panel": noise(streams_of[1], (CHILDREN, CB, PC), (8 * PC) ** -0.5, 0.03125, ((0, 8),)),
        "parent_front": draw_parent_front(jax.random.fold_in(streams_of[5], 71), 0),
        "tile_map": draw_tile_map(jax.random.fold_in(streams_of[5], 71), 0),
        "tile_count": draw_tile_count(jax.random.fold_in(streams_of[5], 71), 0),
    }


def reference(child_front, child_panel, parent_front, tile_map, tile_count):
    highest = lax.Precision.HIGHEST
    pivot_span = STEPS * TILE
    targets = jnp.arange(FT, dtype=jnp.int32)
    front_block = parent_front
    for child_index in range(CHILDREN):
        panel_rows = child_panel[child_index]
        update = child_front[child_index] - lax.dot_general(panel_rows.astype(jnp.float32), panel_rows.astype(jnp.float32), (((1,), (1,)), ((), ())), preferred_element_type=jnp.float32)
        live_tiles = jnp.arange(CT, dtype=jnp.int32) < tile_count[child_index]
        chosen = ((tile_map[child_index][None, :] == targets[:, None]) & live_tiles[None, :]).astype(jnp.float32)
        blocks = update.reshape(CT, TILE, CT, TILE)
        placed = jnp.einsum('ft,taub->faub', chosen, blocks, precision=highest)
        placed = jnp.einsum('faub,gu->fagb', placed, chosen, precision=highest)
        front_block = front_block + placed.reshape(NF, NF)
    factor = jnp.linalg.cholesky(front_block[:pivot_span, :pivot_span])
    below = lax.linalg.triangular_solve(factor, front_block[pivot_span:, :pivot_span], left_side=False, lower=True, transpose_a=True)
    rest = front_block[pivot_span:, pivot_span:] - jnp.dot(below.astype(jnp.float32), below.T.astype(jnp.float32), precision=highest, preferred_element_type=jnp.float32)
    upper_rows = jnp.concatenate([factor, jnp.zeros((pivot_span, NF - pivot_span), jnp.float32)], axis=1)
    lower_rows = jnp.concatenate([below, rest], axis=1)
    return jnp.concatenate([upper_rows, lower_rows], axis=0)
```

```python
import functools

import jax
import jax.numpy as jnp
from jax import lax
from jax.experimental import pallas as pl
from jax.experimental.pallas import tpu as pltpu
from jax.sharding import PartitionSpec as P

TILE = 256
STEPS = 4
SPAN = STEPS * TILE
HIGH = lax.Precision.HIGH


def mm(a, b, dims):
    return lax.dot_general(a, b, (dims, ((), ())), precision=HIGH, preferred_element_type=jnp.float32)


def copy_tile(index, live, src, dst):
    f = pl.program_id(0)

    @pl.when(live[f] > 0)
    def _():
        dst[...] = src[...].reshape(dst.shape)

    @pl.when(live[f] == 0)
    def _():
        dst[...] = jnp.zeros_like(dst)


def place_columns(update, index, live, panels):
    rows = update.shape[0]
    count = index.shape[0]
    per = count // panels
    return pl.pallas_call(
        copy_tile,
        out_shape=jax.ShapeDtypeStruct((panels, rows, per * TILE), jnp.float32),
        grid_spec=pltpu.PrefetchScalarGridSpec(
            num_scalar_prefetch=2,
            grid=(count,),
            in_specs=[pl.BlockSpec((rows, TILE), lambda f, index, live: (0, index[f]))],
            out_specs=pl.BlockSpec((1, rows, TILE), lambda f, index, live: (f // per, 0, f % per)),
        ),
        cost_estimate=pl.CostEstimate(flops=0, bytes_accessed=12 * rows * 2048, transcendentals=0),
    )(index, live, update)


def place_rows(tiles, index, live):
    count = index.shape[0]
    width = tiles.shape[2]
    return pl.pallas_call(
        copy_tile,
        out_shape=jax.ShapeDtypeStruct((count, TILE, width), jnp.float32),
        grid_spec=pltpu.PrefetchScalarGridSpec(
            num_scalar_prefetch=2,
            grid=(count,),
            in_specs=[pl.BlockSpec((1, TILE, width), lambda f, index, live: (index[f], 0, 0))],
            out_specs=pl.BlockSpec((1, TILE, width), lambda f, index, live: (f, 0, 0)),
        ),
        cost_estimate=pl.CostEstimate(flops=0, bytes_accessed=8 * count * TILE * width, transcendentals=0),
    )(index, live, tiles).reshape(count * TILE, width)


def factorize(top):
    eye = jnp.eye(TILE, dtype=jnp.float32)
    work = top
    columns, inverses = [], []
    for _ in range(STEPS):
        diag = jnp.linalg.cholesky(work[:TILE, :TILE])
        inv = lax.linalg.triangular_solve(diag, eye, left_side=True, lower=True)
        lower = mm(work[TILE:, :TILE], inv, ((1,), (1,)))
        work = work[TILE:, TILE:] - mm(lower, lower, ((1,), (1,)))
        columns.append((diag, lower))
        inverses.append(inv)
    return columns, inverses


def shards(child_front, child_panel, parent_front, tile_map, tile_count):
    leaves, panels = lax.axis_size("leaf"), lax.axis_size("panel")
    leaf_id, panel_id = lax.axis_index("leaf"), lax.axis_index("panel")
    child_rows, order = child_front.shape[1:]
    height, width = parent_front.shape
    child_tiles, front_tiles = order // TILE, leaves * height // TILE
    own_tiles = child_rows // TILE
    row_start, col_start = leaf_id * height, panel_id * width
    is_top, is_left = row_start < SPAN, col_start < SPAN

    panel_all = child_panel[0]
    own_panel = lax.dynamic_slice_in_dim(panel_all, panel_id * child_rows, child_rows, 0)
    update = child_front[0] - lax.dot_general(
        own_panel, panel_all, (((1,), (1,)), ((), ())), preferred_element_type=jnp.float32
    )
    targets = jnp.arange(front_tiles, dtype=jnp.int32)
    positions = jnp.arange(child_tiles, dtype=jnp.int32)
    hit = (tile_map[0][None, :] == targets[:, None]) & (positions < tile_count[0])[None, :]
    live = jnp.any(hit, axis=1).astype(jnp.int32)
    index = jnp.sum(jnp.where(hit, positions[None, :], 0), axis=1).astype(jnp.int32)

    placed = place_columns(update, index, live, panels)
    pivot_panels = SPAN // width
    left = jnp.concatenate([placed[i] for i in range(pivot_panels)], axis=1)
    own = index[:STEPS] - panel_id * own_tiles
    held = (live[:STEPS] > 0) & (own >= 0) & (own < own_tiles)
    top_part = place_rows(
        left.reshape(own_tiles, TILE, SPAN),
        jnp.where(held, own, 0).astype(jnp.int32),
        held.astype(jnp.int32),
    )
    own_top = jnp.where(is_top & is_left, parent_front, 0.0)
    row_clip = jnp.where(is_top, row_start, 0)
    col_clip = jnp.where(is_left, col_start, 0)
    old = lax.dynamic_slice(top_part, (row_clip, col_clip), (height, width))
    top_part = lax.dynamic_update_slice(top_part, old + own_top, (row_clip, col_clip))
    top = lax.psum(top_part, ("leaf", "panel"))

    moved = lax.all_to_all(placed, "panel", split_axis=0, concat_axis=0, tiled=True)
    moved = moved.reshape(child_tiles, TILE, width)
    pivot_part = place_rows(moved, index[:STEPS], live[:STEPS])
    old = lax.dynamic_slice(pivot_part, (row_clip, 0), (height, width))
    pivot_part = lax.dynamic_update_slice(
        pivot_part, old + jnp.where(is_top, parent_front, 0.0), (row_clip, 0)
    )
    pivot_rows = lax.psum(pivot_part, "leaf")
    expanded = place_rows(moved, index, live)
    front_block = parent_front + lax.psum_scatter(expanded, "leaf", scatter_dimension=0, tiled=True)

    mine = lax.dynamic_slice(pivot_rows, (0, lax.rem(row_start, width)), (SPAN, height))
    source = [l * height // width for l in range(leaves)]
    own_cols = mine
    for shift in range(1, panels):
        pairs = [
            (l * panels + source[l], l * panels + (source[l] + shift) % panels) for l in range(leaves)
        ]
        got = lax.ppermute(mine, ("leaf", "panel"), pairs)
        holder = row_start // width
        own_cols = jnp.where(lax.rem(holder + shift, panels) == panel_id, got, own_cols)

    columns, inverses = factorize(top)
    rhs = jnp.concatenate([pivot_rows, own_cols], axis=1)
    solved = []
    for k in range(STEPS):
        solved.append(mm(inverses[k], rhs[:TILE], ((1,), (0,))))
        if k < STEPS - 1:
            rhs = rhs[TILE:] - mm(columns[k][1], solved[k], ((1,), (0,)))
    solved = jnp.concatenate(solved, axis=0)
    below_cols, below_rows = solved[:, :width], solved[:, width:]
    rest = front_block - mm(below_rows, below_cols, ((0,), (0,)))

    factor = jnp.concatenate(
        [
            jnp.concatenate([jnp.zeros((k * TILE, TILE), jnp.float32), diag, lower], axis=0)
            for k, (diag, lower) in enumerate(columns)
        ],
        axis=1,
    )
    factor_part = lax.dynamic_slice(factor, (row_clip, col_clip), (height, width))
    below_part = lax.dynamic_slice(below_rows, (col_clip, 0), (width, height)).T
    left_part = jnp.where(is_top, factor_part, below_part)
    right_part = jnp.where(is_top, 0.0, rest)
    return jnp.where(is_left, left_part, right_part)


def solution(mesh):
    placed = (
        P("leaf", "panel", None),
        P("leaf", None, None),
        P("leaf", "panel"),
        P("leaf", None),
        P("leaf"),
    )
    return jax.shard_map(
        shards, mesh=mesh, in_specs=placed, out_specs=P("leaf", "panel"), check_vma=False
    )
```

```python
import functools

import jax
import jax.numpy as jnp
import numpy as np
from jax import lax
from jax.experimental import pallas as pl
from jax.experimental.pallas import tpu as pltpu
from jax.sharding import PartitionSpec as P

TILE = 256
STEPS = 4
SPAN = STEPS * TILE
BLOCK = 128
HIGH = lax.Precision.HIGH


def mm(a, b, dims):
    return lax.dot_general(a, b, (dims, ((), ())), precision=HIGH, preferred_element_type=jnp.float32)


def copy_tile(index, live, src, dst):
    f = pl.program_id(0)

    @pl.when(live[f] > 0)
    def _():
        dst[...] = src[...].reshape(dst.shape)

    @pl.when(live[f] == 0)
    def _():
        dst[...] = jnp.zeros_like(dst)


def place_columns(update, index, live, panels):
    rows = update.shape[0]
    count = index.shape[0]
    per = count // panels
    return pl.pallas_call(
        copy_tile,
        out_shape=jax.ShapeDtypeStruct((panels, rows, per * TILE), jnp.float32),
        grid_spec=pltpu.PrefetchScalarGridSpec(
            num_scalar_prefetch=2,
            grid=(count,),
            in_specs=[pl.BlockSpec((rows, TILE), lambda f, index, live: (0, index[f]))],
            out_specs=pl.BlockSpec((1, rows, TILE), lambda f, index, live: (f // per, 0, f % per)),
        ),
        cost_estimate=pl.CostEstimate(flops=0, bytes_accessed=12 * rows * 2048, transcendentals=0),
    )(index, live, update)


def place_rows(tiles, index, live):
    count = index.shape[0]
    width = tiles.shape[2]
    return pl.pallas_call(
        copy_tile,
        out_shape=jax.ShapeDtypeStruct((count, TILE, width), jnp.float32),
        grid_spec=pltpu.PrefetchScalarGridSpec(
            num_scalar_prefetch=2,
            grid=(count,),
            in_specs=[pl.BlockSpec((1, TILE, width), lambda f, index, live: (index[f], 0, 0))],
            out_specs=pl.BlockSpec((1, TILE, width), lambda f, index, live: (f, 0, 0)),
        ),
        cost_estimate=pl.CostEstimate(flops=0, bytes_accessed=8 * count * TILE * width, transcendentals=0),
    )(index, live, tiles).reshape(count * TILE, width)


def place_parts(tiles, index, part, live, rows):
    count = index.shape[0]
    width = tiles.shape[2]

    def body(index, part, live, src, dst):
        copy_tile(index, live, src, dst)

    return pl.pallas_call(
        body,
        out_shape=jax.ShapeDtypeStruct((count * rows, width), jnp.float32),
        grid_spec=pltpu.PrefetchScalarGridSpec(
            num_scalar_prefetch=3,
            grid=(count,),
            in_specs=[
                pl.BlockSpec((1, rows, width), lambda f, index, part, live: (index[f], part[f], 0))
            ],
            out_specs=pl.BlockSpec((rows, width), lambda f, index, part, live: (f, 0)),
        ),
        cost_estimate=pl.CostEstimate(flops=0, bytes_accessed=8 * count * rows * width, transcendentals=0),
    )(index, part, live, tiles)


def factorize(top):
    eye = jnp.eye(BLOCK, dtype=jnp.float32)
    work = top
    columns, inverses = [], []
    for _ in range(SPAN // BLOCK):
        diag = lax.linalg.cholesky(work[:BLOCK, :BLOCK], symmetrize_input=False)
        inv = lax.linalg.triangular_solve(diag, eye, left_side=True, lower=True)
        lower = mm(work[BLOCK:, :BLOCK], inv, ((1,), (1,)))
        work = work[BLOCK:, BLOCK:] - mm(lower, lower, ((1,), (1,)))
        columns.append((diag, lower))
        inverses.append(inv)
    return columns, inverses


def shards(child_front, child_panel, parent_front, tile_map, tile_count):
    leaves, panels = lax.axis_size("leaf"), lax.axis_size("panel")
    leaf_id, panel_id = lax.axis_index("leaf"), lax.axis_index("panel")
    child_rows, order = child_front.shape[1:]
    height, width = parent_front.shape
    child_tiles, front_tiles = order // TILE, leaves * height // TILE
    own_tiles = child_rows // TILE
    row_start, col_start = leaf_id * height, panel_id * width
    is_top, is_left = row_start < SPAN, col_start < SPAN

    panel_all = child_panel[0]
    own_panel = lax.dynamic_slice_in_dim(panel_all, panel_id * child_rows, child_rows, 0)
    update = child_front[0] - lax.dot_general(
        own_panel, panel_all, (((1,), (1,)), ((), ())), preferred_element_type=jnp.float32
    )
    targets = jnp.arange(front_tiles, dtype=jnp.int32)
    positions = jnp.arange(child_tiles, dtype=jnp.int32)
    hit = (tile_map[0][None, :] == targets[:, None]) & (positions < tile_count[0])[None, :]
    live = jnp.any(hit, axis=1).astype(jnp.int32)
    index = jnp.sum(jnp.where(hit, positions[None, :], 0), axis=1).astype(jnp.int32)

    placed = place_columns(update, index, live, panels)
    row_clip = jnp.where(is_top, row_start, 0)
    col_clip = jnp.where(is_left, col_start, 0)
    moved = lax.all_to_all(placed, "panel", split_axis=0, concat_axis=0, tiled=True)
    moved = moved.reshape(child_tiles, TILE, width)
    pivot_part = place_rows(moved, index[:STEPS], live[:STEPS])
    old = lax.dynamic_slice(pivot_part, (row_clip, 0), (height, width))
    pivot_part = lax.dynamic_update_slice(
        pivot_part, old + jnp.where(is_top, parent_front, 0.0), (row_clip, 0)
    )
    pivot_rows = lax.psum(pivot_part, "leaf")
    tops = SPAN // height
    tail = height * tops // leaves
    head = height - tail
    served = head // tail
    order_rows = []
    for l in range(leaves):
        if l < tops:
            order_rows += [(tops + l * served + i) * height + head for i in range(served)]
        else:
            order_rows += [l * height + i * tail for i in range(served)]
    order_rows = np.array(order_rows)
    expanded = place_parts(
        moved,
        index[order_rows // TILE],
        jnp.asarray(order_rows % TILE // tail, jnp.int32),
        live[order_rows // TILE],
        tail,
    )
    summed = lax.psum_scatter(expanded, "leaf", scatter_dimension=0, tiled=True)
    end = jnp.zeros((tail, width), jnp.float32)
    for i in range(served):
        pairs = [(l, tops + l * served + i) for l in range(tops)]
        got = lax.ppermute(summed[i * tail : (i + 1) * tail], "leaf", pairs)
        end = jnp.where(lax.rem(leaf_id - tops + served * leaves, served) == i, got, end)
    front_block = parent_front + jnp.concatenate([summed, end], axis=0)

    mine = lax.dynamic_slice(pivot_rows, (0, lax.rem(row_start, width)), (SPAN, height))
    source = [l * height // width for l in range(leaves)]
    own_cols = mine
    for shift in range(1, panels):
        pairs = [
            (l * panels + source[l], l * panels + (source[l] + shift) % panels) for l in range(leaves)
        ]
        got = lax.ppermute(mine, ("leaf", "panel"), pairs)
        holder = row_start // width
        own_cols = jnp.where(lax.rem(holder + shift, panels) == panel_id, got, own_cols)

    pieces = []
    for root in range(SPAN // width):
        local = range(width // TILE)
        value = jnp.concatenate(
            [
                pivot_rows[(root * width + k * TILE) :, k * TILE : (k + 1) * TILE]
                for k in local
            ],
            axis=0,
        )
        holders, step = [root], panels // 2
        while step:
            got = lax.ppermute(value, "panel", [(h, h ^ step) for h in holders])
            reached = [h ^ step for h in holders]
            takes = functools.reduce(jnp.logical_or, [panel_id == h for h in reached])
            value = jnp.where(takes, got, value)
            holders, step = holders + reached, step // 2
        at = 0
        for k in local:
            above = root * width + k * TILE
            piece = value[at : at + SPAN - above]
            at += SPAN - above
            pieces.append(jnp.concatenate([jnp.zeros((above, TILE), jnp.float32), piece], axis=0))
    columns, inverses = factorize(jnp.concatenate(pieces, axis=1))
    rhs = jnp.concatenate([pivot_rows, own_cols], axis=1)
    solved = []
    for k, inverse in enumerate(inverses):
        solved.append(mm(inverse, rhs[:BLOCK], ((1,), (0,))))
        if k + 1 < len(inverses):
            rhs = rhs[BLOCK:] - mm(columns[k][1], solved[k], ((1,), (0,)))
    solved = jnp.concatenate(solved, axis=0)
    below_cols, below_rows = solved[:, :width], solved[:, width:]
    rest = front_block - mm(below_rows, below_cols, ((0,), (0,)))

    factor = jnp.concatenate(
        [
            jnp.concatenate([jnp.zeros((k * BLOCK, BLOCK), jnp.float32), diag, lower], axis=0)
            for k, (diag, lower) in enumerate(columns)
        ],
        axis=1,
    )
    factor_part = lax.dynamic_slice(factor, (row_clip, col_clip), (height, width))
    below_part = lax.dynamic_slice(below_rows, (col_clip, 0), (width, height)).T
    left_part = jnp.where(is_top, factor_part, below_part)
    right_part = jnp.where(is_top, 0.0, rest)
    return jnp.where(is_left, left_part, right_part)


def solution(mesh):
    placed = (
        P("leaf", "panel", None),
        P("leaf", None, None),
        P("leaf", "panel"),
        P("leaf", None),
        P("leaf"),
    )
    return jax.shard_map(
        shards, mesh=mesh, in_specs=placed, out_specs=P("leaf", "panel"), check_vma=False
    )
```

```python
import functools

import jax
import jax.numpy as jnp
import numpy as np
from jax import lax
from jax.experimental import pallas as pl
from jax.experimental.pallas import tpu as pltpu
from jax.sharding import PartitionSpec as P

TILE = 256
STEPS = 4
SPAN = STEPS * TILE
BLOCK = 128
HIGH = lax.Precision.HIGH


def mm(a, b, dims):
    return lax.dot_general(a, b, (dims, ((), ())), precision=HIGH, preferred_element_type=jnp.float32)


def copy_tile(index, live, src, dst):
    f = pl.program_id(0)

    @pl.when(live[f] > 0)
    def _():
        dst[...] = src[...].reshape(dst.shape)

    @pl.when(live[f] == 0)
    def _():
        dst[...] = jnp.zeros_like(dst)


def place_columns(update, index, live, panels):
    rows = update.shape[0]
    count = index.shape[0]
    per = count // panels
    return pl.pallas_call(
        copy_tile,
        out_shape=jax.ShapeDtypeStruct((panels, rows, per * TILE), jnp.float32),
        grid_spec=pltpu.PrefetchScalarGridSpec(
            num_scalar_prefetch=2,
            grid=(count,),
            in_specs=[pl.BlockSpec((rows, TILE), lambda f, index, live: (0, index[f]))],
            out_specs=pl.BlockSpec((1, rows, TILE), lambda f, index, live: (f // per, 0, f % per)),
        ),
        cost_estimate=pl.CostEstimate(flops=0, bytes_accessed=12 * rows * 2048, transcendentals=0),
    )(index, live, update)


def place_rows(tiles, index, live):
    count = index.shape[0]
    width = tiles.shape[2]
    return pl.pallas_call(
        copy_tile,
        out_shape=jax.ShapeDtypeStruct((count, TILE, width), jnp.float32),
        grid_spec=pltpu.PrefetchScalarGridSpec(
            num_scalar_prefetch=2,
            grid=(count,),
            in_specs=[pl.BlockSpec((1, TILE, width), lambda f, index, live: (index[f], 0, 0))],
            out_specs=pl.BlockSpec((1, TILE, width), lambda f, index, live: (f, 0, 0)),
        ),
        cost_estimate=pl.CostEstimate(flops=0, bytes_accessed=8 * count * TILE * width, transcendentals=0),
    )(index, live, tiles).reshape(count * TILE, width)


def place_parts(tiles, index, part, live, rows):
    count = index.shape[0]
    width = tiles.shape[2]

    def body(index, part, live, src, dst):
        copy_tile(index, live, src, dst)

    return pl.pallas_call(
        body,
        out_shape=jax.ShapeDtypeStruct((count * rows, width), jnp.float32),
        grid_spec=pltpu.PrefetchScalarGridSpec(
            num_scalar_prefetch=3,
            grid=(count,),
            in_specs=[
                pl.BlockSpec((1, rows, width), lambda f, index, part, live: (index[f], part[f], 0))
            ],
            out_specs=pl.BlockSpec((rows, width), lambda f, index, part, live: (f, 0)),
        ),
        cost_estimate=pl.CostEstimate(flops=0, bytes_accessed=8 * count * rows * width, transcendentals=0),
    )(index, part, live, tiles)


def factorize(top, arrived):
    eye = jnp.eye(BLOCK, dtype=jnp.float32)
    work = top
    columns, inverses = [], []
    for step in range(SPAN // BLOCK):
        if step == SPAN // BLOCK - 1:
            work = jnp.where(arrived == arrived, work, 0.0)
        diag = lax.linalg.cholesky(work[:BLOCK, :BLOCK], symmetrize_input=False)
        inv = lax.linalg.triangular_solve(diag, eye, left_side=True, lower=True)
        lower = mm(work[BLOCK:, :BLOCK], inv, ((1,), (1,)))
        work = work[BLOCK:, BLOCK:] - mm(lower, lower, ((1,), (1,)))
        columns.append((diag, lower))
        inverses.append(inv)
    return columns, inverses


def shards(child_front, child_panel, parent_front, tile_map, tile_count):
    leaves, panels = lax.axis_size("leaf"), lax.axis_size("panel")
    leaf_id, panel_id = lax.axis_index("leaf"), lax.axis_index("panel")
    child_rows, order = child_front.shape[1:]
    height, width = parent_front.shape
    child_tiles, front_tiles = order // TILE, leaves * height // TILE
    own_tiles = child_rows // TILE
    row_start, col_start = leaf_id * height, panel_id * width
    is_top, is_left = row_start < SPAN, col_start < SPAN

    panel_all = child_panel[0]
    own_panel = lax.dynamic_slice_in_dim(panel_all, panel_id * child_rows, child_rows, 0)
    update = child_front[0] - lax.dot_general(
        own_panel, panel_all, (((1,), (1,)), ((), ())), preferred_element_type=jnp.float32
    )
    targets = jnp.arange(front_tiles, dtype=jnp.int32)
    positions = jnp.arange(child_tiles, dtype=jnp.int32)
    hit = (tile_map[0][None, :] == targets[:, None]) & (positions < tile_count[0])[None, :]
    live = jnp.any(hit, axis=1).astype(jnp.int32)
    index = jnp.sum(jnp.where(hit, positions[None, :], 0), axis=1).astype(jnp.int32)

    placed = place_columns(update, index, live, panels)
    row_clip = jnp.where(is_top, row_start, 0)
    col_clip = jnp.where(is_left, col_start, 0)
    moved = lax.all_to_all(placed, "panel", split_axis=0, concat_axis=0, tiled=True)
    moved = moved.reshape(child_tiles, TILE, width)
    pivot_part = place_rows(moved, index[:STEPS], live[:STEPS])
    old = lax.dynamic_slice(pivot_part, (row_clip, 0), (height, width))
    pivot_part = lax.dynamic_update_slice(
        pivot_part, old + jnp.where(is_top, parent_front, 0.0), (row_clip, 0)
    )
    pivot_rows = lax.psum(pivot_part, "leaf")
    tops = SPAN // height
    tail = height * tops // leaves
    head = height - tail
    served = head // tail
    order_rows = []
    for l in range(leaves):
        if l < tops:
            order_rows += [(tops + l * served + i) * height + head for i in range(served)]
        else:
            order_rows += [l * height + i * tail for i in range(served)]
    order_rows = np.array(order_rows)
    expanded = place_parts(
        moved,
        index[order_rows // TILE],
        jnp.asarray(order_rows % TILE // tail, jnp.int32),
        live[order_rows // TILE],
        tail,
    )
    summed = lax.psum_scatter(expanded, "leaf", scatter_dimension=0, tiled=True)
    end = jnp.zeros((tail, width), jnp.float32)
    for i in range(served):
        pairs = [(l, tops + l * served + i) for l in range(tops)]
        got = lax.ppermute(summed[i * tail : (i + 1) * tail], "leaf", pairs)
        end = jnp.where(lax.rem(leaf_id - tops + served * leaves, served) == i, got, end)
    front_block = parent_front + jnp.concatenate([summed, end], axis=0)

    pieces = []
    for root in range(SPAN // width):
        local = range(width // TILE)
        value = jnp.concatenate(
            [
                pivot_rows[(root * width + k * TILE) :, k * TILE : (k + 1) * TILE]
                for k in local
            ],
            axis=0,
        )
        holders, step = [root], panels // 2
        while step:
            got = lax.ppermute(value, "panel", [(h, h ^ step) for h in holders])
            reached = [h ^ step for h in holders]
            takes = functools.reduce(jnp.logical_or, [panel_id == h for h in reached])
            value = jnp.where(takes, got, value)
            holders, step = holders + reached, step // 2
        at = 0
        for k in local:
            above = root * width + k * TILE
            piece = value[at : at + SPAN - above]
            at += SPAN - above
            pieces.append(jnp.concatenate([jnp.zeros((above, TILE), jnp.float32), piece], axis=0))
    columns, inverses = factorize(jnp.concatenate(pieces, axis=1), end[0, 0])
    mine = lax.dynamic_slice(pivot_rows, (0, lax.rem(row_start, width)), (SPAN, height))
    source = [l * height // width for l in range(leaves)]
    mine = jnp.where(columns[0][0][0, 0] > 0, mine, 0.0)
    own_cols = mine
    for shift in range(1, panels):
        pairs = [
            (l * panels + source[l], l * panels + (source[l] + shift) % panels) for l in range(leaves)
        ]
        got = lax.ppermute(mine, ("leaf", "panel"), pairs)
        holder = row_start // width
        own_cols = jnp.where(lax.rem(holder + shift, panels) == panel_id, got, own_cols)

    rhs = jnp.concatenate([pivot_rows, own_cols], axis=1)
    solved = []
    for k, inverse in enumerate(inverses):
        solved.append(mm(inverse, rhs[:BLOCK], ((1,), (0,))))
        if k + 1 < len(inverses):
            rhs = rhs[BLOCK:] - mm(columns[k][1], solved[k], ((1,), (0,)))
    solved = jnp.concatenate(solved, axis=0)
    below_cols, below_rows = solved[:, :width], solved[:, width:]
    rest = front_block - mm(below_rows, below_cols, ((0,), (0,)))

    factor = jnp.concatenate(
        [
            jnp.concatenate([jnp.zeros((k * BLOCK, BLOCK), jnp.float32), diag, lower], axis=0)
            for k, (diag, lower) in enumerate(columns)
        ],
        axis=1,
    )
    factor_part = lax.dynamic_slice(factor, (row_clip, col_clip), (height, width))
    below_part = lax.dynamic_slice(below_rows, (col_clip, 0), (width, height)).T
    left_part = jnp.where(is_top, factor_part, below_part)
    right_part = jnp.where(is_top, 0.0, rest)
    return jnp.where(is_left, left_part, right_part)


def solution(mesh):
    placed = (
        P("leaf", "panel", None),
        P("leaf", None, None),
        P("leaf", "panel"),
        P("leaf", None),
        P("leaf"),
    )
    return jax.shard_map(
        shards, mesh=mesh, in_specs=placed, out_specs=P("leaf", "panel"), check_vma=False
    )
```
